256 devices in a mesh: cls: 2 (over x_lo), row: 128 (over z, x_hi, y, core).
Axes of the slice: x: 4 (x_hi: 2, x_lo: 2; x = x_hi * 2 + x_lo), y: 4, z: 8, core: 2. Of those that a mesh axis runs over, the one named last changes fastest.
Arguments:
- coeffs: bfloat16 [2, 1, 8192, 8192], P('cls', None, 'row'), may hold values from -6 to 6
- h_blocks: bfloat16 [2, 128, 64, 256], P('cls'), may hold values from -0.375 to 0.375
- h_cols: int32 [2, 128, 4], P('cls'), may hold values from 0 to 127, all different within a row
- g_blocks: bfloat16 [2, 128, 64, 128], P('cls'), may hold values from -0.5 to 0.5
- g_cols: int32 [2, 128, 2], P('cls'), may hold values from 0 to 127, all different within a row
Outputs:
- sigma_out: bfloat16 [2, 1, 8192, 8192], P('cls', None, 'row')
The draws below stay inside these ranges and needn't reach their ends.
Inputs may be any that keep to these rules, and one draw needn't show every extreme that they name: `h_cols`: each block row names 4 different block columns, and every block column is named in at least one of the two classes. `g_cols`: each block row names 2 different block columns, and every block column is named in at least one of the two classes.
All inputs are finite; a program needn't handle non-finite values.
Results may differ from the reference program's by a relative error of at most 0.0043.
Values may be sent and summed in bfloat16 or wider, within the bound.
A program may use at most 128 MiB of HBM per device.

```python
import jax
import jax.numpy as jnp
from jax import lax

BLK = 64
ROOTS = 1
KH = 4
KG = 2
NBLK = 128
N = 8192


def shard_levels(rng, extent, pieces, smallest, top_value):
    def one(dim, parts):
        heights = jax.random.uniform(jax.random.fold_in(jax.random.fold_in(rng, 6), dim), (parts,), jnp.float32, smallest / len(pieces), top_value / len(pieces))
        return jnp.repeat(jnp.exp(heights), extent[dim] // parts).reshape((-1,) + (1,) * (len(extent) - dim - 1))

    level = one(*pieces[0])
    for cut in pieces[1:]:
        level = level * one(*cut)
    return level


def different_ones(rng, rows, amount, top, lift):
    sequence = jax.random.permutation(jax.random.fold_in(rng, 1), amount)
    boost = sequence
    for power in range(3):
        boost = boost * boost // amount
    boost = boost * lift // amount
    lots = jax.random.randint(jax.random.fold_in(rng, 2), (rows, amount), 0, 4096) + boost
    holders = jax.random.permutation(jax.random.fold_in(rng, 3), rows)[jnp.arange(amount) % rows]
    lots = jnp.where(jnp.arange(rows)[:, None] == holders[None, :], 1 << 14, lots)
    score = lots * amount + jnp.arange(amount)
    return lax.top_k(score.astype(jnp.int32), top)[1].astype(jnp.int32)


def normal_values(own_key, dims, scale, reach, split=(), kind=jnp.bfloat16):
    values = jax.random.normal(own_key, dims, jnp.float32) * scale
    if len(split) > 0:
        values = shard_levels(own_key, dims, split, -0.22, 0.18) * values
    return jnp.clip(values, min=-reach, max=reach).astype(kind)


def setup_inputs(seed: int = 0) -> dict:
    streams_of = jax.random.split(jax.random.key(seed), 6)
    coeffs = normal_values(streams_of[0], (2, ROOTS, N, N), 1.0, 6.0, ((0, 2), (2, 128)))
    h_blocks = normal_values(streams_of[1], (2, NBLK, BLK, KH * BLK), (KH * BLK) ** -0.5, 0.375, ((0, 2),))
    h_cols = different_ones(streams_of[2], 2 * NBLK, NBLK, KH, 0).reshape((2, NBLK, KH))
    g_blocks = normal_values(streams_of[3], (2, NBLK, BLK, KG * BLK), (KG * BLK) ** -0.5, 0.5, ((0, 2),))
    g_cols = different_ones(streams_of[4], 2 * NBLK, NBLK, KG, 128).reshape((2, NBLK, KG))
    return dict(coeffs=coeffs, h_blocks=h_blocks, h_cols=h_cols, g_blocks=g_blocks, g_cols=g_cols)


def reference(coeffs, h_blocks, h_cols, g_blocks, g_cols):
    results = []
    for c in range(2):
        own_class = coeffs[c]
        other_class = coeffs[1 - c]

        def beta_row(row_block):
            running = jnp.zeros((ROOTS, N, BLK), jnp.float32)
            for k in range(KH):
                start = (h_cols[c, row_block, k] * BLK).astype(jnp.int32)
                column_piece = lax.dynamic_slice_in_dim(own_class, start, BLK, 2)
                block = h_blocks[c, row_block, :, k * BLK:(k + 1) * BLK]
                running = running + jnp.einsum('raj,oj->rao', column_piece.astype(jnp.float32), block.astype(jnp.float32))
            return running

        def alpha_row(row_block):
            running = jnp.zeros((ROOTS, BLK, N), jnp.float32)
            for k in range(KH):
                start = (h_cols[c, row_block, k] * BLK).astype(jnp.int32)
                row_piece = lax.dynamic_slice_in_dim(own_class, start, BLK, 1)
                block = h_blocks[c, row_block, :, k * BLK:(k + 1) * BLK]
                running = running + jnp.einsum('oj,rjb->rob', block.astype(jnp.float32), row_piece.astype(jnp.float32))
            for k in range(KG):
                start = (g_cols[c, row_block, k] * BLK).astype(jnp.int32)
                row_piece = lax.dynamic_slice_in_dim(other_class, start, BLK, 1)
                block = g_blocks[c, row_block, :, k * BLK:(k + 1) * BLK]
                running = running + jnp.einsum('oj,rjb->rob', block.astype(jnp.float32), row_piece.astype(jnp.float32))
            return running

        indices = jnp.arange(NBLK, dtype=jnp.int32)
        beta_term = lax.map(beta_row, indices)
        beta_term = jnp.transpose(beta_term, (1, 2, 0, 3)).reshape(ROOTS, N, N)
        alpha_term = lax.map(alpha_row, indices)
        alpha_term = jnp.transpose(alpha_term, (1, 0, 2, 3)).reshape(ROOTS, N, N).astype(jnp.bfloat16)
        results.append((beta_term + alpha_term.astype(jnp.float32)).astype(jnp.bfloat16))
    return jnp.stack(results)
```

```python
import functools

import jax
import jax.numpy as jnp
from jax import lax
from jax.experimental import pallas as pl
from jax.experimental.pallas import tpu as pltpu
from jax.sharding import PartitionSpec as P

MESH = pl.DeviceIdType.MESH
NY = 4
BLK = 64
LANES = 128
KH = 4
KG = 2


def hop(k, nz):
    return lax.rem(((k + 1) // 2) * (2 * lax.rem(k, 2) - 1) + nz, nz)


def kernel(nz, ny, c_ref, h_hbm, hc, g_hbm, gc, out_ref, slabs, halves, own, other, prod, back, beta, hv, gv,
           load_sem, s1_send, s1_recv, x_send, x_recv, sib_recv, r_send, r_recv):
    chips = nz * 2 * ny
    plane = 2 * ny
    cls, row = lax.axis_index("cls"), lax.axis_index("row")
    core, p = lax.rem(row, 2), row // 2
    z, xh, y = p // plane, lax.rem(p // ny, 2), lax.rem(p, ny)

    def device(c, z_, xh_, y_, s_):
        return (c, ((z_ * 2 + xh_) * ny + y_) * 2 + s_)

    pair = device(1 - cls, z, xh, y, core)
    side = device(1 - cls, z, 1 - xh, y, core)
    across = device(cls, z, 1 - xh, y, core)
    sibling = device(cls, z, xh, y, 1 - core)

    h_copy = pltpu.make_async_copy(h_hbm.at[0], hv, load_sem.at[0])
    g_copy = pltpu.make_async_copy(g_hbm.at[0], gv, load_sem.at[1])
    h_copy.start()
    g_copy.start()

    barrier = pltpu.get_barrier_semaphore()

    @pl.loop(1, chips)
    def _(i):
        pl.semaphore_signal(barrier, inc=1, device_id=(cls, lax.rem(p + i, chips) * 2 + core), device_id_type=MESH)

    for target in (pair, side, sibling):
        pl.semaphore_signal(barrier, inc=1, device_id=target, device_id_type=MESH)
    pl.semaphore_wait(barrier, chips + 2)

    def remote(src, dst, send, recv, target):
        return pltpu.make_async_remote_copy(
            src_ref=src, dst_ref=dst, send_sem=send, recv_sem=recv, device_id=target, device_id_type=MESH)

    mine = z * ny + y

    @pl.loop(0, nz)
    def _(k):
        to_z = lax.rem(z + hop(k, nz), nz)
        for a in range(2):
            for b in range(ny):
                start = pl.multiple_of(((to_z * 2 + a) * ny + b) * LANES, LANES)
                slabs[to_z * plane + b * 2 + a] = c_ref[0, 0, :, pl.ds(start, LANES)]
        for d in range(ny):
            to_y = lax.rem(y + d, ny)
            src = pl.ds(to_z * plane + to_y * 2, 2)

            def send():
                remote(slabs.at[src], own.at[pl.ds(core * 3 + xh, 2), mine], s1_send.at[k], s1_recv.at[k],
                       device(cls, to_z, xh, to_y, core)).start()

            if d == 0:
                pl.when(k > 0)(send)
            else:
                send()

    own[core * 3 + xh, mine] = slabs[z * plane + y * 2]
    own[core * 3 + xh + 1, mine] = slabs[z * plane + y * 2 + 1]

    low = lax.broadcasted_iota(jnp.int32, (BLK, LANES), 1) < BLK

    @pl.loop(0, chips)
    def _(t):
        wide = c_ref[0, 0, :, pl.ds(pl.multiple_of(t * LANES, LANES), LANES)].astype(jnp.float32)
        turned = pltpu.roll(wide, BLK, 1)
        zero = jnp.zeros_like(wide)
        halves[0, 2 * t] = jnp.where(low, wide, zero).astype(jnp.bfloat16)
        halves[1, 2 * t + 1] = jnp.where(low, zero, wide).astype(jnp.bfloat16)
        halves[0, 2 * t + 1] = jnp.where(low, turned, zero).astype(jnp.bfloat16)
        halves[1, 2 * t] = jnp.where(low, zero, turned).astype(jnp.bfloat16)

    h_copy.wait()

    def beta_slab(q):
        tall = []
        for i in (2 * q, 2 * q + 1):
            wide = [halves[0, hc[0, i, k]] + halves[1, hc[0, i, k + 1]] for k in range(0, KH, 2)]
            tall.append(jnp.concatenate(wide, axis=1))
        blocks = hv[pl.ds(2 * q, 2)].reshape(2 * BLK, KH * BLK)
        both = lax.dot_general(jnp.concatenate(tall, axis=0), blocks, (((1,), (1,)), ((), ())),
                               preferred_element_type=jnp.float32)
        beta[q] = jnp.where(low, both[:BLK], both[BLK:])

    def group(k):
        return pl.ds(lax.rem(z - hop(k, nz) + nz, nz) * ny, ny)

    def forward(k):
        zs = group(k)
        arrived = (other.at[core * 2 + xh, zs], other.at[core * 2 + 1 - xh, zs], own.at[core * 3 + 2 * (1 - xh), zs])
        for n, ref in enumerate(arrived):
            remote(ref, ref, x_send.at[n], x_recv.at[n, k], sibling).wait_recv()
            remote(ref, ref, x_send.at[4 + n], sib_recv.at[1 + n], sibling).start()

    @pl.loop(0, nz)
    def _(k):
        zs = group(k)

        @pl.when(k == 0)
        def _():
            part = own.at[pl.ds(core * 3 + xh, 2), pl.ds(0, ny - 1)]
            remote(part, part, s1_send.at[k], s1_recv.at[k], sibling).wait_recv()

        @pl.when(k > 0)
        def _():
            part = own.at[pl.ds(core * 3 + xh, 2), zs]
            remote(part, part, s1_send.at[k], s1_recv.at[k], sibling).wait_recv()

        straight, transit = own.at[core * 3 + 2 * xh, zs], own.at[core * 3 + 1, zs]
        remote(straight, other.at[core * 2 + xh, zs], x_send.at[0], x_recv.at[0, k], pair).start()
        remote(transit, other.at[core * 2 + xh, zs], x_send.at[1], x_recv.at[1, k], side).start()
        remote(transit, straight, x_send.at[2], x_recv.at[2, k], across).start()
        remote(straight, straight, x_send.at[3], sib_recv.at[0], sibling).start()
        for i in range(plane):
            beta_slab(k * plane + i)

        @pl.when(k > 0)
        def _():
            forward(k - 1)

    forward(nz - 1)
    g_copy.wait()
    theirs = (own.at[(1 - core) * 3 + 2 * xh], other.at[(1 - core) * 2 + xh], other.at[(1 - core) * 2 + 1 - xh],
              own.at[(1 - core) * 3 + 2 * (1 - xh)])
    for n, ref in enumerate(theirs):
        remote(ref, ref, x_send.at[0], sib_recv.at[n], sibling).wait_recv()

    def place(j):
        s, q = lax.rem(j, 2), j // 2
        return s, lax.rem(q // ny, 2), (q // plane) * ny + lax.rem(q, ny)

    def own_rows(j):
        s, a, b = place(j)
        return own[s * 3 + 2 * a, b]

    def other_rows(j):
        s, a, b = place(j)
        return other[s * 2 + a, b]

    def alpha_block(q):
        i = 2 * q + core
        x = jnp.concatenate([own_rows(hc[0, i, k]) for k in range(KH)], axis=0)
        w = jnp.concatenate([other_rows(gc[0, i, k]) for k in range(KG)], axis=0)
        total = jnp.dot(hv[i], x, preferred_element_type=jnp.float32)
        total = total + jnp.dot(gv[i], w, preferred_element_type=jnp.float32)
        prod[q] = total.astype(jnp.bfloat16)

    @pl.loop(0, nz)
    def _(k):
        n = nz - 1 - k
        to_z = lax.rem(z + hop(n, nz), nz)
        for i in range(plane):
            alpha_block(to_z * plane + i)
        for i in range(plane):
            q = to_z * plane + i

            @pl.when(q != p)
            def _():
                remote(prod.at[q], back.at[p], r_send, r_recv.at[n], (cls, 2 * q + core)).start()

            @pl.when(q == p)
            def _():
                back[p] = prod[p]

    @pl.loop(0, nz)
    def _(k):
        n = nz - 1 - k
        from_z = lax.rem(z - hop(n, nz) + nz, nz)

        @pl.when(n == 0)
        def _():
            part = back.at[pl.ds(0, plane - 1)]
            remote(part, part, r_send, r_recv.at[n], sibling).wait_recv()

        @pl.when(n > 0)
        def _():
            part = back.at[pl.ds(from_z * plane, plane)]
            remote(part, part, r_send, r_recv.at[n], sibling).wait_recv()

        for i in range(plane):
            q = from_z * plane + i
            total = beta[q] + back[q].astype(jnp.float32)
            out_ref[0, 0, :, pl.ds(pl.multiple_of(q * LANES, LANES), LANES)] = total.astype(jnp.bfloat16)

    @pl.loop(0, nz)
    def _(k):
        @pl.when(k == 0)
        def _():
            part = slabs.at[pl.ds(0, 2 * (ny - 1))]
            remote(part, part, s1_send.at[k], s1_recv.at[k], sibling).wait_send()

        @pl.when(k > 0)
        def _():
            part = slabs.at[pl.ds(0, plane)]
            remote(part, part, s1_send.at[k], s1_recv.at[k], sibling).wait_send()

    for n in range(7):
        remote(own.at[0], own.at[0], x_send.at[n], sib_recv.at[0], sibling).wait_send()
    part = prod.at[pl.ds(0, chips - 1)]
    remote(part, part, r_send, r_recv.at[0], sibling).wait_send()


def per_device(ny, coeffs, h_blocks, h_cols, g_blocks, g_cols):
    num_blocks = h_cols.shape[1]
    chips = num_blocks // 2
    nz = chips // (2 * ny)
    bf16, dma = jnp.bfloat16, pltpu.SemaphoreType.DMA
    vmem, smem = pl.BlockSpec(memory_space=pltpu.VMEM), pl.BlockSpec(memory_space=pltpu.SMEM)
    hbm = pl.BlockSpec(memory_space=pl.ANY)
    return pl.pallas_call(
        functools.partial(kernel, nz, ny),
        out_shape=jax.ShapeDtypeStruct(coeffs.shape, bf16),
        in_specs=[vmem, hbm, smem, hbm, smem],
        out_specs=vmem,
        scratch_shapes=[
            pltpu.VMEM((chips, BLK, LANES), bf16),
            pltpu.VMEM((2, num_blocks, BLK, LANES), bf16),
            pltpu.VMEM((6, nz * ny, BLK, LANES), bf16),
            pltpu.VMEM((4, nz * ny, BLK, LANES), bf16),
            pltpu.VMEM((chips, BLK, LANES), bf16),
            pltpu.VMEM((chips, BLK, LANES), bf16),
            pltpu.VMEM((chips, BLK, LANES), jnp.float32),
            pltpu.VMEM(h_blocks.shape[1:], bf16),
            pltpu.VMEM(g_blocks.shape[1:], bf16),
            dma((2,)), dma((nz,)), dma((nz,)), dma((7,)), dma((3, nz)), dma((4,)), dma, dma((nz,)),
        ],
        compiler_params=pltpu.CompilerParams(collective_id=0, has_side_effects=True, vmem_limit_bytes=48 * 2**20),
        cost_estimate=pl.CostEstimate(flops=670_000_000, bytes_accessed=9 * 2**20, transcendentals=0),
    )(coeffs, h_blocks, h_cols, g_blocks, g_cols)


def solution(mesh, ny=NY):
    return jax.shard_map(
        functools.partial(per_device, ny),
        mesh=mesh,
        in_specs=(
            P("cls", None, "row", None),
            P("cls", None, None, None),
            P("cls", None, None),
            P("cls", None, None, None),
            P("cls", None, None),
        ),
        out_specs=P("cls", None, "row", None),
        check_vma=False,
    )
```

```python
import functools

import jax
import jax.numpy as jnp
from jax import lax
from jax.experimental import pallas as pl
from jax.experimental.pallas import tpu as pltpu
from jax.sharding import PartitionSpec as P

MESH = pl.DeviceIdType.MESH
NY = 4
BLK = 64
LANES = 128
KH = 4
KG = 2
DEPTH = 8


def hop(k, nz):
    return lax.rem(((k + 1) // 2) * (2 * lax.rem(k, 2) - 1) + nz, nz)


def kernel(nz, ny, c_hbm, h_hbm, hc, g_hbm, gc, out_ref, rows, slabs, halves, own, other, prod, back, beta, hv, gv,
           load_sem, enter_sem, s1_send, s1_recv, x_send, x_recv, sib_recv, r_send, r_recv):
    chips = nz * 2 * ny
    plane = 2 * ny
    cls, row = lax.axis_index("cls"), lax.axis_index("row")
    core, p = lax.rem(row, 2), row // 2
    z, xh, y = p // plane, lax.rem(p // ny, 2), lax.rem(p, ny)

    def device(c, z_, xh_, y_, s_):
        return (c, ((z_ * 2 + xh_) * ny + y_) * 2 + s_)

    pair = device(1 - cls, z, xh, y, core)
    side = device(1 - cls, z, 1 - xh, y, core)
    across = device(cls, z, 1 - xh, y, core)
    sibling = device(cls, z, xh, y, 1 - core)

    c_copy = pltpu.make_async_copy(c_hbm.at[0, 0], rows, load_sem.at[0])
    h_copy = pltpu.make_async_copy(h_hbm.at[0], hv, load_sem.at[1])
    g_copy = pltpu.make_async_copy(g_hbm.at[0], gv, load_sem.at[2])
    c_copy.start()
    h_copy.start()
    g_copy.start()

    barrier = pltpu.get_barrier_semaphore()
    along_y = [device(cls, z, xh, lax.rem(y + d, ny), core) for d in range(1, ny)]
    along_z = [device(cls, lax.rem(z + d, nz), xh, y, core) for d in range(1, nz)]
    for target in [pair, side, across, sibling] + along_y + along_z:
        pl.semaphore_signal(barrier, inc=1, device_id=target, device_id_type=MESH)

    c_copy.wait()

    @pl.loop(0, nz * 2)
    def _(i):
        for b in range(ny):
            start = pl.multiple_of((i * ny + b) * LANES, LANES)
            slabs[(i // 2) * plane + b * 2 + lax.rem(i, 2)] = rows[:, pl.ds(start, LANES)]

    pl.semaphore_wait(barrier, ny + nz + 2)
    for target in along_y:
        pl.semaphore_signal(enter_sem, inc=1, device_id=target, device_id_type=MESH)
    pl.semaphore_wait(enter_sem, ny - 1)

    def remote(src, dst, send, recv, target):
        return pltpu.make_async_remote_copy(
            src_ref=src, dst_ref=dst, send_sem=send, recv_sem=recv, device_id=target, device_id_type=MESH)

    mine = z * ny + y

    def scatter(k):
        to_z = lax.rem(z + hop(k, nz), nz)
        for d in range(ny):
            to_y = lax.rem(y + d, ny)
            src = pl.ds(to_z * plane + to_y * 2, 2)

            def send():
                remote(slabs.at[src], own.at[pl.ds(core * 3 + xh, 2), mine], s1_send.at[k], s1_recv.at[k],
                       device(cls, to_z, xh, to_y, core)).start()

            if d == 0:
                pl.when(k > 0)(send)
            else:
                send()

    @pl.loop(0, DEPTH)
    def _(k):
        scatter(k)

    own[core * 3 + xh, mine] = slabs[z * plane + y * 2]
    own[core * 3 + xh + 1, mine] = slabs[z * plane + y * 2 + 1]

    low = lax.broadcasted_iota(jnp.int32, (BLK, LANES), 1) < BLK

    @pl.loop(0, chips)
    def _(t):
        wide = rows[:, pl.ds(pl.multiple_of(t * LANES, LANES), LANES)].astype(jnp.float32)
        turned = pltpu.roll(wide, BLK, 1)
        zero = jnp.zeros_like(wide)
        halves[0, 2 * t] = jnp.where(low, wide, zero).astype(jnp.bfloat16)
        halves[1, 2 * t + 1] = jnp.where(low, zero, wide).astype(jnp.bfloat16)
        halves[0, 2 * t + 1] = jnp.where(low, turned, zero).astype(jnp.bfloat16)
        halves[1, 2 * t] = jnp.where(low, zero, turned).astype(jnp.bfloat16)

    h_copy.wait()

    def beta_slab(q):
        tall = []
        for i in (2 * q, 2 * q + 1):
            wide = [halves[0, hc[0, k, i]] + halves[1, hc[0, k + 1, i]] for k in range(0, KH, 2)]
            tall.append(jnp.concatenate(wide, axis=1))
        blocks = hv[pl.ds(2 * q, 2)].reshape(2 * BLK, KH * BLK)
        both = lax.dot_general(jnp.concatenate(tall, axis=0), blocks, (((1,), (1,)), ((), ())),
                               preferred_element_type=jnp.float32)
        beta[q] = jnp.where(low, both[:BLK], both[BLK:])

    def group(k):
        return pl.ds(lax.rem(z - hop(k, nz) + nz, nz) * ny, ny)

    def forward(k):
        zs = group(k)
        arrived = (other.at[core * 2 + xh, zs], other.at[core * 2 + 1 - xh, zs], own.at[core * 3 + 2 * (1 - xh), zs])
        for n, ref in enumerate(arrived):
            remote(ref, ref, x_send.at[n], x_recv.at[n, k], sibling).wait_recv()
            remote(ref, ref, x_send.at[4 + n], sib_recv.at[1 + n], sibling).start()

    @pl.loop(0, nz)
    def _(k):
        zs = group(k)

        @pl.when(k == 0)
        def _():
            part = own.at[pl.ds(core * 3 + xh, 2), pl.ds(0, ny - 1)]
            remote(part, part, s1_send.at[k], s1_recv.at[k], sibling).wait_recv()

        @pl.when(k > 0)
        def _():
            part = own.at[pl.ds(core * 3 + xh, 2), zs]
            remote(part, part, s1_send.at[k], s1_recv.at[k], sibling).wait_recv()

        straight, transit = own.at[core * 3 + 2 * xh, zs], own.at[core * 3 + 1, zs]
        remote(straight, other.at[core * 2 + xh, zs], x_send.at[0], x_recv.at[0, k], pair).start()
        remote(transit, other.at[core * 2 + xh, zs], x_send.at[1], x_recv.at[1, k], side).start()
        remote(transit, straight, x_send.at[2], x_recv.at[2, k], across).start()
        remote(straight, straight, x_send.at[3], sib_recv.at[0], sibling).start()
        @pl.when(k + DEPTH < nz)
        def _():
            scatter(k + DEPTH)

        for i in range(plane):
            beta_slab(k * plane + i)

        @pl.when(k > 0)
        def _():
            forward(k - 1)

    forward(nz - 1)
    g_copy.wait()
    theirs = (own.at[(1 - core) * 3 + 2 * xh], other.at[(1 - core) * 2 + xh], other.at[(1 - core) * 2 + 1 - xh],
              own.at[(1 - core) * 3 + 2 * (1 - xh)])
    for n, ref in enumerate(theirs):
        remote(ref, ref, x_send.at[0], sib_recv.at[n], sibling).wait_recv()

    def place(j):
        s, q = lax.rem(j, 2), j // 2
        return s, lax.rem(q // ny, 2), (q // plane) * ny + lax.rem(q, ny)

    def own_rows(j):
        s, a, b = place(j)
        return own[s * 3 + 2 * a, b]

    def other_rows(j):
        s, a, b = place(j)
        return other[s * 2 + a, b]

    def alpha_block(q):
        i = 2 * q + core
        x = jnp.concatenate([own_rows(hc[0, k, i]) for k in range(KH)], axis=0)
        w = jnp.concatenate([other_rows(gc[0, k, i]) for k in range(KG)], axis=0)
        total = jnp.dot(hv[i], x, preferred_element_type=jnp.float32)
        total = total + jnp.dot(gv[i], w, preferred_element_type=jnp.float32)
        prod[q] = total.astype(jnp.bfloat16)

    @pl.loop(0, nz)
    def _(k):
        n = nz - 1 - k
        to_z = lax.rem(z + hop(n, nz), nz)
        for i in range(plane):
            alpha_block(to_z * plane + i)
        for i in range(plane):
            q = to_z * plane + i

            @pl.when(q != p)
            def _():
                remote(prod.at[q], back.at[p], r_send, r_recv.at[n], (cls, 2 * q + core)).start()

            @pl.when(q == p)
            def _():
                back[p] = prod[p]

    @pl.loop(0, nz)
    def _(k):
        n = nz - 1 - k
        from_z = lax.rem(z - hop(n, nz) + nz, nz)

        @pl.when(n == 0)
        def _():
            part = back.at[pl.ds(0, plane - 1)]
            remote(part, part, r_send, r_recv.at[n], sibling).wait_recv()

        @pl.when(n > 0)
        def _():
            part = back.at[pl.ds(from_z * plane, plane)]
            remote(part, part, r_send, r_recv.at[n], sibling).wait_recv()

        for i in range(plane):
            q = from_z * plane + i
            total = beta[q] + back[q].astype(jnp.float32)
            out_ref[0, 0, :, pl.ds(pl.multiple_of(q * LANES, LANES), LANES)] = total.astype(jnp.bfloat16)

    @pl.loop(0, nz)
    def _(k):
        @pl.when(k == 0)
        def _():
            part = slabs.at[pl.ds(0, 2 * (ny - 1))]
            remote(part, part, s1_send.at[k], s1_recv.at[k], sibling).wait_send()

        @pl.when(k > 0)
        def _():
            part = slabs.at[pl.ds(0, plane)]
            remote(part, part, s1_send.at[k], s1_recv.at[k], sibling).wait_send()

    for n in range(7):
        remote(own.at[0], own.at[0], x_send.at[n], sib_recv.at[0], sibling).wait_send()
    part = prod.at[pl.ds(0, chips - 1)]
    remote(part, part, r_send, r_recv.at[0], sibling).wait_send()


def per_device(ny, coeffs, h_blocks, h_cols, g_blocks, g_cols):
    num_blocks = h_cols.shape[1]
    chips = num_blocks // 2
    nz = chips // (2 * ny)
    bf16, dma = jnp.bfloat16, pltpu.SemaphoreType.DMA
    vmem, smem = pl.BlockSpec(memory_space=pltpu.VMEM), pl.BlockSpec(memory_space=pltpu.SMEM)
    hbm = pl.BlockSpec(memory_space=pl.ANY)
    return pl.pallas_call(
        functools.partial(kernel, nz, ny),
        out_shape=jax.ShapeDtypeStruct(coeffs.shape, bf16),
        in_specs=[hbm, hbm, smem, hbm, smem],
        out_specs=vmem,
        scratch_shapes=[
            pltpu.VMEM(coeffs.shape[2:], bf16),
            pltpu.VMEM((chips, BLK, LANES), bf16),
            pltpu.VMEM((2, num_blocks, BLK, LANES), bf16),
            pltpu.VMEM((6, nz * ny, BLK, LANES), bf16),
            pltpu.VMEM((4, nz * ny, BLK, LANES), bf16),
            pltpu.VMEM((chips, BLK, LANES), bf16),
            pltpu.VMEM((chips, BLK, LANES), bf16),
            pltpu.VMEM((chips, BLK, LANES), jnp.float32),
            pltpu.VMEM(h_blocks.shape[1:], bf16),
            pltpu.VMEM(g_blocks.shape[1:], bf16),
            dma((3,)), pltpu.SemaphoreType.REGULAR, dma((nz,)), dma((nz,)), dma((7,)), dma((3, nz)), dma((4,)), dma, dma((nz,)),
        ],
        compiler_params=pltpu.CompilerParams(collective_id=0, has_side_effects=True, vmem_limit_bytes=62 * 2**20),
        cost_estimate=pl.CostEstimate(flops=670_000_000, bytes_accessed=9 * 2**20, transcendentals=0),
    )(coeffs, h_blocks, jnp.swapaxes(h_cols, 1, 2), g_blocks, jnp.swapaxes(g_cols, 1, 2))


def solution(mesh, ny=NY):
    return jax.shard_map(
        functools.partial(per_device, ny),
        mesh=mesh,
        in_specs=(
            P("cls", None, "row", None),
            P("cls", None, None, None),
            P("cls", None, None),
            P("cls", None, None, None),
            P("cls", None, None),
        ),
        out_specs=P("cls", None, "row", None),
        check_vma=False,
    )
```

```python
import functools

import jax
import jax.numpy as jnp
from jax import lax
from jax.experimental import pallas as pl
from jax.experimental.pallas import tpu as pltpu
from jax.sharding import PartitionSpec as P

MESH = pl.DeviceIdType.MESH
NY = 4
BLK = 64
LANES = 128
KH = 4
KG = 2


def hop(k, nz):
    if isinstance(k, int):
        return ((k + 1) // 2 * (2 * (k % 2) - 1)) % nz
    return lax.rem(((k + 1) // 2) * (2 * lax.rem(k, 2) - 1) + nz, nz)


def kernel(nz, ny, c_hbm, h_hbm, hc, g_hbm, gc, out_ref, rows, slabs, halves, own, other, prod, back, beta, hv, gv,
           load_sem, enter_sem, z_send, z_recv, x_send, x_recv, sib_recv, r_send, r_recv):
    chips = nz * 2 * ny
    plane = 2 * ny
    cls, row = lax.axis_index("cls"), lax.axis_index("row")
    core, p = lax.rem(row, 2), row // 2
    z, xh, y = p // plane, lax.rem(p // ny, 2), lax.rem(p, ny)

    def device(c, z_, xh_, y_, s_):
        return (c, ((z_ * 2 + xh_) * ny + y_) * 2 + s_)

    pair = device(1 - cls, z, xh, y, core)
    side = device(1 - cls, z, 1 - xh, y, core)
    across = device(cls, z, 1 - xh, y, core)
    sibling = device(cls, z, xh, y, 1 - core)

    c_copy = pltpu.make_async_copy(c_hbm.at[0, 0], rows, load_sem.at[0])
    h_copy = pltpu.make_async_copy(h_hbm.at[0], hv, load_sem.at[1])
    g_copy = pltpu.make_async_copy(g_hbm.at[0], gv, load_sem.at[2])
    c_copy.start()
    h_copy.start()
    g_copy.start()

    barrier = pltpu.get_barrier_semaphore()
    along_y = [device(cls, z, xh, lax.rem(y + d, ny), core) for d in range(1, ny)]
    along_z = [device(cls, lax.rem(z + d, nz), xh, y, core) for d in range(1, nz)]
    for target in [pair, side, across, sibling] + along_y + along_z:
        pl.semaphore_signal(barrier, inc=1, device_id=target, device_id_type=MESH)

    c_copy.wait()

    def cut(half):
        @pl.loop(0, nz)
        def _(i):
            for b in range(ny):
                q = (i * 2 + half) * ny + b
                slabs[q] = rows[:, pl.ds(pl.multiple_of(q * LANES, LANES), LANES)]

    cut(1 - xh)
    pl.semaphore_wait(barrier, ny + nz + 2)
    for target in along_y:
        pl.semaphore_signal(enter_sem, inc=1, device_id=target, device_id_type=MESH)

    def remote(src, dst, send, recv, target):
        return pltpu.make_async_remote_copy(
            src_ref=src, dst_ref=dst, send_sem=send, recv_sem=recv, device_id=target, device_id_type=MESH)

    mine = z * ny + y

    def slab(half, kind, k, d):
        to_z, to_y = lax.rem(z + hop(k, nz), nz), lax.rem(y + d, ny)
        row = core * 3 + (1 if kind == 0 else 2 * xh)
        remote(slabs.at[(to_z * 2 + half) * ny + to_y], own.at[row, mine], z_send.at[kind], z_recv.at[kind, k],
               device(cls, to_z, xh, to_y, core)).start()

    for d in range(1, ny):
        slab(1 - xh, 0, 0, d)

    @pl.loop(1, nz)
    def _(k):
        slab(1 - xh, 0, k, 0)

    pl.semaphore_wait(enter_sem, ny - 1)

    for ks in [range(k, min(k + 2, nz)) for k in range(1, nz, 2)]:
        for d in range(1, ny):
            for k in ks:
                slab(1 - xh, 0, k, d)

    cut(xh)
    for d in range(1, ny):
        slab(xh, 1, 0, d)

    for ks in [range(k, min(k + 2, nz)) for k in range(1, nz, 2)]:
        for d in range(ny):
            for k in ks:
                slab(xh, 1, k, d)

    own[core * 3 + 1, mine] = slabs[(z * 2 + 1 - xh) * ny + y]
    own[core * 3 + 2 * xh, mine] = slabs[(z * 2 + xh) * ny + y]

    low = lax.broadcasted_iota(jnp.int32, (BLK, LANES), 1) < BLK

    def halve(t):
        wide = rows[:, pl.ds(pl.multiple_of(t * LANES, LANES), LANES)].astype(jnp.float32)
        turned = pltpu.roll(wide, BLK, 1)
        zero = jnp.zeros_like(wide)
        halves[0, 2 * t] = jnp.where(low, wide, zero).astype(jnp.bfloat16)
        halves[1, 2 * t + 1] = jnp.where(low, zero, wide).astype(jnp.bfloat16)
        halves[0, 2 * t + 1] = jnp.where(low, turned, zero).astype(jnp.bfloat16)
        halves[1, 2 * t] = jnp.where(low, zero, turned).astype(jnp.bfloat16)

    def beta_slab(q):
        tall = []
        for i in (2 * q, 2 * q + 1):
            wide = [halves[0, hc[0, k, i]] + halves[1, hc[0, k + 1, i]] for k in range(0, KH, 2)]
            tall.append(jnp.concatenate(wide, axis=1))
        blocks = hv[pl.ds(2 * q, 2)].reshape(2 * BLK, KH * BLK)
        both = lax.dot_general(jnp.concatenate(tall, axis=0), blocks, (((1,), (1,)), ((), ())),
                               preferred_element_type=jnp.float32)
        beta[q] = jnp.where(low, both[:BLK], both[BLK:])

    def group(k):
        return pl.ds(lax.rem(z - hop(k, nz) + nz, nz) * ny, ny)

    def arrived(kind, k):
        row = core * 3 + (1 if kind == 0 else 2 * xh)

        @pl.when(k == 0)
        def _():
            part = own.at[row, pl.ds(0, ny - 1)]
            remote(part, part, z_send.at[kind], z_recv.at[kind, k], sibling).wait_recv()

        @pl.when(k > 0)
        def _():
            part = own.at[row, group(k)]
            remote(part, part, z_send.at[kind], z_recv.at[kind, k], sibling).wait_recv()

    def forward(n, ref, k):
        remote(ref, ref, x_send.at[n], x_recv.at[n, k], sibling).wait_recv()
        remote(ref, ref, x_send.at[4 + n], sib_recv.at[1 + n], sibling).start()

    def forward_pair(k):
        forward(0, other.at[core * 2 + xh, group(k)], k)

    @pl.loop(0, nz)
    def _(k):
        zs = group(k)
        arrived(0, k)
        transit = own.at[core * 3 + 1, zs]
        remote(transit, other.at[core * 2 + xh, zs], x_send.at[1], x_recv.at[1, k], side).start()
        remote(transit, own.at[core * 3 + 2 * xh, zs], x_send.at[2], x_recv.at[2, k], across).start()
        for i in range(plane):
            halve(k * plane + i)

    h_copy.wait()

    @pl.loop(0, nz)
    def _(k):
        zs = group(k)
        arrived(1, k)
        straight = own.at[core * 3 + 2 * xh, zs]
        remote(straight, other.at[core * 2 + xh, zs], x_send.at[0], x_recv.at[0, k], pair).start()
        remote(straight, straight, x_send.at[3], sib_recv.at[0], sibling).start()
        forward(1, other.at[core * 2 + 1 - xh, zs], k)
        forward(2, own.at[core * 3 + 2 * (1 - xh), zs], k)
        for i in range(plane):
            beta_slab(k * plane + i)

        @pl.when(k > 0)
        def _():
            forward_pair(k - 1)

    forward_pair(nz - 1)
    g_copy.wait()
    theirs = (own.at[(1 - core) * 3 + 2 * xh], other.at[(1 - core) * 2 + xh], other.at[(1 - core) * 2 + 1 - xh],
              own.at[(1 - core) * 3 + 2 * (1 - xh)])
    for n, ref in enumerate(theirs):
        remote(ref, ref, x_send.at[0], sib_recv.at[n], sibling).wait_recv()

    def place(j):
        s, q = lax.rem(j, 2), j // 2
        return s, lax.rem(q // ny, 2), (q // plane) * ny + lax.rem(q, ny)

    def own_rows(j):
        s, a, b = place(j)
        return own[s * 3 + 2 * a, b]

    def other_rows(j):
        s, a, b = place(j)
        return other[s * 2 + a, b]

    def alpha_block(q):
        i = 2 * q + core
        x = jnp.concatenate([own_rows(hc[0, k, i]) for k in range(KH)], axis=0)
        w = jnp.concatenate([other_rows(gc[0, k, i]) for k in range(KG)], axis=0)
        total = jnp.dot(hv[i], x, preferred_element_type=jnp.float32)
        total = total + jnp.dot(gv[i], w, preferred_element_type=jnp.float32)
        prod[q] = total.astype(jnp.bfloat16)

    @pl.loop(0, plane)
    def _(i):
        xy = lax.rem(p + i + 1, plane)
        targets = [(n, lax.rem(z + hop(n, nz), nz) * plane + xy) for n in range(nz - 1, -1, -1)]
        for _, q in targets:
            alpha_block(q)
        for n, q in targets:

            @pl.when(q != p)
            def _():
                remote(prod.at[q], back.at[p], r_send, r_recv.at[n], (cls, 2 * q + core)).start()

            @pl.when(q == p)
            def _():
                back[p] = prod[p]

    @pl.loop(0, nz)
    def _(k):
        n = nz - 1 - k
        from_z = lax.rem(z - hop(n, nz) + nz, nz)

        @pl.when(n == 0)
        def _():
            part = back.at[pl.ds(0, plane - 1)]
            remote(part, part, r_send, r_recv.at[n], sibling).wait_recv()

        @pl.when(n > 0)
        def _():
            part = back.at[pl.ds(from_z * plane, plane)]
            remote(part, part, r_send, r_recv.at[n], sibling).wait_recv()

        for i in range(plane):
            q = from_z * plane + i
            total = beta[q] + back[q].astype(jnp.float32)
            out_ref[0, 0, :, pl.ds(pl.multiple_of(q * LANES, LANES), LANES)] = total.astype(jnp.bfloat16)

    for kind in range(2):
        part = slabs.at[pl.ds(0, nz * ny - 1)]
        remote(part, part, z_send.at[kind], z_recv.at[kind, 0], sibling).wait_send()
    for n in range(7):
        remote(own.at[0], own.at[0], x_send.at[n], sib_recv.at[0], sibling).wait_send()
    part = prod.at[pl.ds(0, chips - 1)]
    remote(part, part, r_send, r_recv.at[0], sibling).wait_send()


def per_device(ny, coeffs, h_blocks, h_cols, g_blocks, g_cols):
    num_blocks = h_cols.shape[1]
    chips = num_blocks // 2
    nz = chips // (2 * ny)
    bf16, dma = jnp.bfloat16, pltpu.SemaphoreType.DMA
    vmem, smem = pl.BlockSpec(memory_space=pltpu.VMEM), pl.BlockSpec(memory_space=pltpu.SMEM)
    hbm = pl.BlockSpec(memory_space=pltpu.HBM)
    return pl.pallas_call(
        functools.partial(kernel, nz, ny),
        out_shape=jax.ShapeDtypeStruct(coeffs.shape, bf16),
        in_specs=[hbm, hbm, smem, hbm, smem],
        out_specs=vmem,
        scratch_shapes=[
            pltpu.VMEM(coeffs.shape[2:], bf16),
            pltpu.VMEM((chips, BLK, LANES), bf16),
            pltpu.VMEM((2, num_blocks, BLK, LANES), bf16),
            pltpu.VMEM((6, nz * ny, BLK, LANES), bf16),
            pltpu.VMEM((4, nz * ny, BLK, LANES), bf16),
            pltpu.VMEM((chips, BLK, LANES), bf16),
            pltpu.VMEM((chips, BLK, LANES), bf16),
            pltpu.VMEM((chips, BLK, LANES), jnp.float32),
            pltpu.VMEM(h_blocks.shape[1:], bf16),
            pltpu.VMEM(g_blocks.shape[1:], bf16),
            dma((3,)), pltpu.SemaphoreType.REGULAR, dma((2,)), dma((2, nz)), dma((7,)), dma((3, nz)), dma((4,)), dma, dma((nz,)),
        ],
        compiler_params=pltpu.CompilerParams(collective_id=0, has_side_effects=True, vmem_limit_bytes=52 * 2**20),
        cost_estimate=pl.CostEstimate(flops=670_000_000, bytes_accessed=9 * 2**20, transcendentals=0),
    )(coeffs, h_blocks, jnp.swapaxes(h_cols, 1, 2), g_blocks, jnp.swapaxes(g_cols, 1, 2))


def solution(mesh, ny=NY):
    return jax.shard_map(
        functools.partial(per_device, ny),
        mesh=mesh,
        in_specs=(
            P("cls", None, "row", None),
            P("cls", None, None, None),
            P("cls", None, None),
            P("cls", None, None, None),
            P("cls", None, None),
        ),
        out_specs=P("cls", None, "row", None),
        check_vma=False,
    )
```

```python
import functools

import jax
import jax.numpy as jnp
from jax import lax
from jax.experimental import pallas as pl
from jax.experimental.pallas import tpu as pltpu
from jax.sharding import PartitionSpec as P

MESH = pl.DeviceIdType.MESH
NY = 4
BLK = 64
LANES = 128
KH = 4
KG = 2


def hop(k, nz):
    if isinstance(k, int):
        return ((k + 1) // 2 * (2 * (k % 2) - 1)) % nz
    return lax.rem(((k + 1) // 2) * (2 * lax.rem(k, 2) - 1) + nz, nz)


def kernel(nz, ny, c_hbm, h_hbm, hc, g_hbm, gc, out_ref, rows, slabs, halves, own, other, prod, back, beta, hv, gv,
           load_sem, enter_sem, z_send, z_recv, x_send, x_recv, sib_recv, r_send, r_recv):
    chips = nz * 2 * ny
    plane = 2 * ny
    cls, row = lax.axis_index("cls"), lax.axis_index("row")
    core, p = lax.rem(row, 2), row // 2
    z, xh, y = p // plane, lax.rem(p // ny, 2), lax.rem(p, ny)

    def device(c, z_, xh_, y_, s_):
        return (c, ((z_ * 2 + xh_) * ny + y_) * 2 + s_)

    pair = device(1 - cls, z, xh, y, core)
    side = device(1 - cls, z, 1 - xh, y, core)
    across = device(cls, z, 1 - xh, y, core)
    sibling = device(cls, z, xh, y, 1 - core)

    c_copy = pltpu.make_async_copy(c_hbm.at[0, 0], rows, load_sem.at[0])
    h_copy = pltpu.make_async_copy(h_hbm.at[0], hv, load_sem.at[1])
    g_copy = pltpu.make_async_copy(g_hbm.at[0], gv, load_sem.at[2])
    c_copy.start()
    h_copy.start()
    g_copy.start()

    barrier = pltpu.get_barrier_semaphore()
    along_y = [device(cls, z, xh, lax.rem(y + d, ny), core) for d in range(1, ny)]
    along_z = [device(cls, lax.rem(z + d, nz), xh, y, core) for d in range(1, nz)]
    for target in [pair, side, across, sibling] + along_y + along_z:
        pl.semaphore_signal(barrier, inc=1, device_id=target, device_id_type=MESH)

    c_copy.wait()

    def cut(half):
        @pl.loop(0, nz)
        def _(i):
            for b in range(ny):
                q = (i * 2 + half) * ny + b
                slabs[q] = rows[:, pl.ds(pl.multiple_of(q * LANES, LANES), LANES)]

    cut(1 - xh)
    pl.semaphore_wait(barrier, ny + nz + 2)
    for target in along_y:
        pl.semaphore_signal(enter_sem, inc=1, device_id=target, device_id_type=MESH)

    def remote(src, dst, send, recv, target):
        return pltpu.make_async_remote_copy(
            src_ref=src, dst_ref=dst, send_sem=send, recv_sem=recv, device_id=target, device_id_type=MESH)

    mine = z * ny + y

    def slab(half, kind, k, d):
        to_z, to_y = lax.rem(z + hop(k, nz), nz), lax.rem(y + d, ny)
        row = core * 3 + (1 if kind == 0 else 2 * xh)
        remote(slabs.at[(to_z * 2 + half) * ny + to_y], own.at[row, mine], z_send.at[kind], z_recv.at[kind, k],
               device(cls, to_z, xh, to_y, core)).start()

    for d in range(1, ny):
        slab(1 - xh, 0, 0, d)

    @pl.loop(1, nz)
    def _(k):
        slab(1 - xh, 0, k, 0)

    pl.semaphore_wait(enter_sem, ny - 1)

    for ks in [range(k, min(k + 2, nz)) for k in range(1, nz, 2)]:
        for d in range(1, ny):
            for k in ks:
                slab(1 - xh, 0, k, d)

    cut(xh)
    for d in range(1, ny):
        slab(xh, 1, 0, d)

    for ks in [range(k, min(k + 2, nz)) for k in range(1, nz, 2)]:
        for d in range(ny):
            for k in ks:
                slab(xh, 1, k, d)

    own[core * 3 + 1, mine] = slabs[(z * 2 + 1 - xh) * ny + y]
    own[core * 3 + 2 * xh, mine] = slabs[(z * 2 + xh) * ny + y]

    low = lax.broadcasted_iota(jnp.int32, (BLK, LANES), 1) < BLK

    def halve(t):
        wide = rows[:, pl.ds(pl.multiple_of(t * LANES, LANES), LANES)].astype(jnp.float32)
        turned = pltpu.roll(wide, BLK, 1)
        zero = jnp.zeros_like(wide)
        halves[0, 2 * t] = jnp.where(low, wide, zero).astype(jnp.bfloat16)
        halves[1, 2 * t + 1] = jnp.where(low, zero, wide).astype(jnp.bfloat16)
        halves[0, 2 * t + 1] = jnp.where(low, turned, zero).astype(jnp.bfloat16)
        halves[1, 2 * t] = jnp.where(low, zero, turned).astype(jnp.bfloat16)

    def beta_slab(q):
        tall = []
        for i in (2 * q, 2 * q + 1):
            wide = [halves[0, hc[0, k, i]] + halves[1, hc[0, k + 1, i]] for k in range(0, KH, 2)]
            tall.append(jnp.concatenate(wide, axis=1))
        blocks = hv[pl.ds(2 * q, 2)].reshape(2 * BLK, KH * BLK)
        both = lax.dot_general(jnp.concatenate(tall, axis=0), blocks, (((1,), (1,)), ((), ())),
                               preferred_element_type=jnp.float32)
        beta[q] = jnp.where(low, both[:BLK], both[BLK:])

    def group(k):
        return pl.ds(lax.rem(z - hop(k, nz) + nz, nz) * ny, ny)

    def arrived(kind, k):
        row = core * 3 + (1 if kind == 0 else 2 * xh)

        @pl.when(k == 0)
        def _():
            part = own.at[row, pl.ds(0, ny - 1)]
            remote(part, part, z_send.at[kind], z_recv.at[kind, k], sibling).wait_recv()

        @pl.when(k > 0)
        def _():
            part = own.at[row, group(k)]
            remote(part, part, z_send.at[kind], z_recv.at[kind, k], sibling).wait_recv()

    def forward(n, ref, k):
        remote(ref, ref, x_send.at[n], x_recv.at[n, k], sibling).wait_recv()
        remote(ref, ref, x_send.at[4 + n], sib_recv.at[1 + n], sibling).start()

    @pl.loop(0, nz)
    def _(k):
        zs = group(k)
        arrived(0, k)
        transit = own.at[core * 3 + 1, zs]
        remote(transit, other.at[core * 2 + xh, zs], x_send.at[1], x_recv.at[1, k], side).start()
        remote(transit, own.at[core * 3 + 2 * xh, zs], x_send.at[2], x_recv.at[2, k], across).start()
        for i in range(plane):
            halve(k * plane + i)

    h_copy.wait()

    @pl.loop(0, nz)
    def _(k):
        zs = group(k)
        arrived(1, k)
        straight = own.at[core * 3 + 2 * xh, zs]
        remote(straight, other.at[core * 2 + xh, zs], x_send.at[0], x_recv.at[0, k], pair).start()
        remote(straight, straight, x_send.at[3], sib_recv.at[0], sibling).start()
        for i in range(plane):
            beta_slab(k * plane + i)

    @pl.loop(0, nz)
    def _(k):
        forward(1, other.at[core * 2 + 1 - xh, group(k)], k)
        forward(2, own.at[core * 3 + 2 * (1 - xh), group(k)], k)

    @pl.loop(0, nz)
    def _(k):
        forward(0, other.at[core * 2 + xh, group(k)], k)

    g_copy.wait()
    theirs = (own.at[(1 - core) * 3 + 2 * xh], other.at[(1 - core) * 2 + xh], other.at[(1 - core) * 2 + 1 - xh],
              own.at[(1 - core) * 3 + 2 * (1 - xh)])
    for n, ref in enumerate(theirs):
        remote(ref, ref, x_send.at[0], sib_recv.at[n], sibling).wait_recv()

    def place(j):
        s, q = lax.rem(j, 2), j // 2
        return s, lax.rem(q // ny, 2), (q // plane) * ny + lax.rem(q, ny)

    def own_rows(j):
        s, a, b = place(j)
        return own[s * 3 + 2 * a, b]

    def other_rows(j):
        s, a, b = place(j)
        return other[s * 2 + a, b]

    def alpha_block(q):
        i = 2 * q + core
        x = jnp.concatenate([own_rows(hc[0, k, i]) for k in range(KH)], axis=0)
        w = jnp.concatenate([other_rows(gc[0, k, i]) for k in range(KG)], axis=0)
        total = jnp.dot(hv[i], x, preferred_element_type=jnp.float32)
        total = total + jnp.dot(gv[i], w, preferred_element_type=jnp.float32)
        prod[q] = total.astype(jnp.bfloat16)

    @pl.loop(0, plane)
    def _(i):
        xy = lax.rem(p + i + 1, plane)
        targets = [(n, lax.rem(z + hop(n, nz), nz) * plane + xy) for n in range(nz - 1, -1, -1)]
        for _, q in targets:
            alpha_block(q)
        for n, q in targets:

            @pl.when(q != p)
            def _():
                remote(prod.at[q], back.at[p], r_send, r_recv.at[n], (cls, 2 * q + core)).start()

            @pl.when(q == p)
            def _():
                back[p] = prod[p]

    @pl.loop(0, nz)
    def _(k):
        n = nz - 1 - k
        from_z = lax.rem(z - hop(n, nz) + nz, nz)

        @pl.when(n == 0)
        def _():
            part = back.at[pl.ds(0, plane - 1)]
            remote(part, part, r_send, r_recv.at[n], sibling).wait_recv()

        @pl.when(n > 0)
        def _():
            part = back.at[pl.ds(from_z * plane, plane)]
            remote(part, part, r_send, r_recv.at[n], sibling).wait_recv()

        for i in range(plane):
            q = from_z * plane + i
            total = beta[q] + back[q].astype(jnp.float32)
            out_ref[0, 0, :, pl.ds(pl.multiple_of(q * LANES, LANES), LANES)] = total.astype(jnp.bfloat16)

    for kind in range(2):
        part = slabs.at[pl.ds(0, nz * ny - 1)]
        remote(part, part, z_send.at[kind], z_recv.at[kind, 0], sibling).wait_send()
    for n in range(7):
        remote(own.at[0], own.at[0], x_send.at[n], sib_recv.at[0], sibling).wait_send()
    part = prod.at[pl.ds(0, chips - 1)]
    remote(part, part, r_send, r_recv.at[0], sibling).wait_send()


def per_device(ny, coeffs, h_blocks, h_cols, g_blocks, g_cols):
    num_blocks = h_cols.shape[1]
    chips = num_blocks // 2
    nz = chips // (2 * ny)
    bf16, dma = jnp.bfloat16, pltpu.SemaphoreType.DMA
    vmem, smem = pl.BlockSpec(memory_space=pltpu.VMEM), pl.BlockSpec(memory_space=pltpu.SMEM)
    hbm = pl.BlockSpec(memory_space=pltpu.HBM)
    return pl.pallas_call(
        functools.partial(kernel, nz, ny),
        out_shape=jax.ShapeDtypeStruct(coeffs.shape, bf16),
        in_specs=[hbm, hbm, smem, hbm, smem],
        out_specs=vmem,
        scratch_shapes=[
            pltpu.VMEM(coeffs.shape[2:], bf16),
            pltpu.VMEM((chips, BLK, LANES), bf16),
            pltpu.VMEM((2, num_blocks, BLK, LANES), bf16),
            pltpu.VMEM((6, nz * ny, BLK, LANES), bf16),
            pltpu.VMEM((4, nz * ny, BLK, LANES), bf16),
            pltpu.VMEM((chips, BLK, LANES), bf16),
            pltpu.VMEM((chips, BLK, LANES), bf16),
            pltpu.VMEM((chips, BLK, LANES), jnp.float32),
            pltpu.VMEM(h_blocks.shape[1:], bf16),
            pltpu.VMEM(g_blocks.shape[1:], bf16),
            dma((3,)), pltpu.SemaphoreType.REGULAR, dma((2,)), dma((2, nz)), dma((7,)), dma((3, nz)), dma((4,)), dma, dma((nz,)),
        ],
        compiler_params=pltpu.CompilerParams(collective_id=0, has_side_effects=True, vmem_limit_bytes=52 * 2**20),
        cost_estimate=pl.CostEstimate(flops=670_000_000, bytes_accessed=9 * 2**20, transcendentals=0),
    )(coeffs, h_blocks, jnp.swapaxes(h_cols, 1, 2), g_blocks, jnp.swapaxes(g_cols, 1, 2))


def solution(mesh, ny=NY):
    return jax.shard_map(
        functools.partial(per_device, ny),
        mesh=mesh,
        in_specs=(
            P("cls", None, "row", None),
            P("cls", None, None, None),
            P("cls", None, None),
            P("cls", None, None, None),
            P("cls", None, None),
        ),
        out_specs=P("cls", None, "row", None),
        check_vma=False,
    )
```

```python
import functools

import jax
import jax.numpy as jnp
from jax import lax
from jax.experimental import pallas as pl
from jax.experimental.pallas import tpu as pltpu
from jax.sharding import PartitionSpec as P

MESH = pl.DeviceIdType.MESH
NY = 4
BLK = 64
LANES = 128
KH = 4
KG = 2


def hop(k, nz):
    if isinstance(k, int):
        return ((k + 1) // 2 * (2 * (k % 2) - 1)) % nz
    return lax.rem(((k + 1) // 2) * (2 * lax.rem(k, 2) - 1) + nz, nz)


def kernel(nz, ny, c_hbm, h_hbm, hc, g_hbm, gc, out_ref, rows, slabs, halves, own, other, prod, back, beta, hv, gv,
           load_sem, enter_sem, z_send, z_recv, x_send, x_recv, sib_recv, r_send, r_recv):
    chips = nz * 2 * ny
    plane = 2 * ny
    cls, row = lax.axis_index("cls"), lax.axis_index("row")
    core, p = lax.rem(row, 2), row // 2
    z, xh, y = p // plane, lax.rem(p // ny, 2), lax.rem(p, ny)

    def device(c, z_, xh_, y_, s_):
        return (c, ((z_ * 2 + xh_) * ny + y_) * 2 + s_)

    pair = device(1 - cls, z, xh, y, core)
    side = device(1 - cls, z, 1 - xh, y, core)
    across = device(cls, z, 1 - xh, y, core)
    sibling = device(cls, z, xh, y, 1 - core)

    c_copy = pltpu.make_async_copy(c_hbm.at[0, 0], rows, load_sem.at[0])
    h_copy = pltpu.make_async_copy(h_hbm.at[0], hv, load_sem.at[1])
    g_copy = pltpu.make_async_copy(g_hbm.at[0], gv, load_sem.at[2])
    c_copy.start()
    h_copy.start()
    g_copy.start()

    barrier = pltpu.get_barrier_semaphore()
    along_y = [device(cls, z, xh, lax.rem(y + d, ny), core) for d in range(1, ny)]
    along_z = [device(cls, lax.rem(z + d, nz), xh, y, core) for d in range(1, nz)]
    for target in [pair, side, across, sibling] + along_y + along_z:
        pl.semaphore_signal(barrier, inc=1, device_id=target, device_id_type=MESH)

    c_copy.wait()

    def cut(half):
        @pl.loop(0, nz)
        def _(i):
            for b in range(ny):
                q = (i * 2 + half) * ny + b
                slabs[q] = rows[:, pl.ds(pl.multiple_of(q * LANES, LANES), LANES)]

    cut(1 - xh)
    pl.semaphore_wait(barrier, ny + nz + 2)
    for target in along_y:
        pl.semaphore_signal(enter_sem, inc=1, device_id=target, device_id_type=MESH)

    def remote(src, dst, send, recv, target):
        return pltpu.make_async_remote_copy(
            src_ref=src, dst_ref=dst, send_sem=send, recv_sem=recv, device_id=target, device_id_type=MESH)

    mine = z * ny + y
    far_y = sorted(range(1, ny), key=lambda d: -min(d, ny - d))

    def slab(half, kind, k, d):
        to_z, to_y = lax.rem(z + hop(k, nz), nz), lax.rem(y + d, ny)
        row = core * 3 + (1 if kind == 0 else 2 * xh)
        remote(slabs.at[(to_z * 2 + half) * ny + to_y], own.at[row, mine], z_send.at[kind], z_recv.at[kind, k],
               device(cls, to_z, xh, to_y, core)).start()

    for d in range(1, ny):
        slab(1 - xh, 0, 0, d)

    @pl.loop(1, nz)
    def _(k):
        slab(1 - xh, 0, k, 0)

    pl.semaphore_wait(enter_sem, ny - 1)

    for ks in [range(k, min(k + 2, nz)) for k in range(1, nz, 2)]:
        for d in far_y:
            for k in ks:
                slab(1 - xh, 0, k, d)

    cut(xh)
    for d in range(1, ny):
        slab(xh, 1, 0, d)

    for ks in [range(k, min(k + 2, nz)) for k in range(1, nz, 2)]:
        for d in far_y + [0]:
            for k in ks:
                slab(xh, 1, k, d)

    own[core * 3 + 1, mine] = slabs[(z * 2 + 1 - xh) * ny + y]
    own[core * 3 + 2 * xh, mine] = slabs[(z * 2 + xh) * ny + y]

    low = lax.broadcasted_iota(jnp.int32, (BLK, LANES), 1) < BLK

    def halve(t):
        wide = rows[:, pl.ds(pl.multiple_of(t * LANES, LANES), LANES)].astype(jnp.float32)
        turned = pltpu.roll(wide, BLK, 1)
        zero = jnp.zeros_like(wide)
        halves[0, 2 * t] = jnp.where(low, wide, zero).astype(jnp.bfloat16)
        halves[1, 2 * t + 1] = jnp.where(low, zero, wide).astype(jnp.bfloat16)
        halves[0, 2 * t + 1] = jnp.where(low, turned, zero).astype(jnp.bfloat16)
        halves[1, 2 * t] = jnp.where(low, zero, turned).astype(jnp.bfloat16)

    def beta_slab(q):
        tall = []
        for i in (2 * q, 2 * q + 1):
            wide = [halves[0, hc[0, k, i]] + halves[1, hc[0, k + 1, i]] for k in range(0, KH, 2)]
            tall.append(jnp.concatenate(wide, axis=1))
        blocks = hv[pl.ds(2 * q, 2)].reshape(2 * BLK, KH * BLK)
        both = lax.dot_general(jnp.concatenate(tall, axis=0), blocks, (((1,), (1,)), ((), ())),
                               preferred_element_type=jnp.float32)
        beta[q] = jnp.where(low, both[:BLK], both[BLK:])

    def group(k):
        return pl.ds(lax.rem(z - hop(k, nz) + nz, nz) * ny, ny)

    def arrived(kind, k):
        row = core * 3 + (1 if kind == 0 else 2 * xh)

        @pl.when(k == 0)
        def _():
            part = own.at[row, pl.ds(0, ny - 1)]
            remote(part, part, z_send.at[kind], z_recv.at[kind, k], sibling).wait_recv()

        @pl.when(k > 0)
        def _():
            part = own.at[row, group(k)]
            remote(part, part, z_send.at[kind], z_recv.at[kind, k], sibling).wait_recv()

    def forward(n, ref, k):
        remote(ref, ref, x_send.at[n], x_recv.at[n, k], sibling).wait_recv()
        remote(ref, ref, x_send.at[4 + n], sib_recv.at[1 + n], sibling).start()

    @pl.loop(0, nz)
    def _(k):
        zs = group(k)
        arrived(0, k)
        transit = own.at[core * 3 + 1, zs]
        remote(transit, other.at[core * 2 + xh, zs], x_send.at[1], x_recv.at[1, k], side).start()
        remote(transit, own.at[core * 3 + 2 * xh, zs], x_send.at[2], x_recv.at[2, k], across).start()
        for i in range(plane):
            halve(k * plane + i)

    h_copy.wait()

    @pl.loop(0, nz)
    def _(k):
        zs = group(k)
        arrived(1, k)
        straight = own.at[core * 3 + 2 * xh, zs]
        remote(straight, other.at[core * 2 + xh, zs], x_send.at[0], x_recv.at[0, k], pair).start()
        remote(straight, straight, x_send.at[3], sib_recv.at[0], sibling).start()
        for i in range(plane):
            beta_slab(k * plane + i)

    @pl.loop(0, nz)
    def _(k):
        forward(1, other.at[core * 2 + 1 - xh, group(k)], k)
        forward(2, own.at[core * 3 + 2 * (1 - xh), group(k)], k)

    @pl.loop(0, nz)
    def _(k):
        forward(0, other.at[core * 2 + xh, group(k)], k)

    g_copy.wait()
    theirs = (own.at[(1 - core) * 3 + 2 * xh], other.at[(1 - core) * 2 + xh], other.at[(1 - core) * 2 + 1 - xh],
              own.at[(1 - core) * 3 + 2 * (1 - xh)])
    for n, ref in enumerate(theirs):
        remote(ref, ref, x_send.at[0], sib_recv.at[n], sibling).wait_recv()

    def place(j):
        s, q = lax.rem(j, 2), j // 2
        return s, lax.rem(q // ny, 2), (q // plane) * ny + lax.rem(q, ny)

    def own_rows(j):
        s, a, b = place(j)
        return own[s * 3 + 2 * a, b]

    def other_rows(j):
        s, a, b = place(j)
        return other[s * 2 + a, b]

    def alpha_block(q):
        i = 2 * q + core
        x = jnp.concatenate([own_rows(hc[0, k, i]) for k in range(KH)], axis=0)
        w = jnp.concatenate([other_rows(gc[0, k, i]) for k in range(KG)], axis=0)
        total = jnp.dot(hv[i], x, preferred_element_type=jnp.float32)
        total = total + jnp.dot(gv[i], w, preferred_element_type=jnp.float32)
        prod[q] = total.astype(jnp.bfloat16)

    @pl.loop(0, plane)
    def _(i):
        xy = lax.rem(p + i + 1, plane)
        targets = [(n, lax.rem(z + hop(n, nz), nz) * plane + xy) for n in range(nz - 1, -1, -1)]
        for part in (targets[: nz // 2], targets[nz // 2 :]):
            for _, q in part:
                alpha_block(q)
            for n, q in part:

                @pl.when(q != p)
                def _():
                    remote(prod.at[q], back.at[p], r_send, r_recv.at[n], (cls, 2 * q + core)).start()

                @pl.when(q == p)
                def _():
                    back[p] = prod[p]

    @pl.loop(0, nz)
    def _(k):
        n = nz - 1 - k
        from_z = lax.rem(z - hop(n, nz) + nz, nz)

        @pl.when(n == 0)
        def _():
            part = back.at[pl.ds(0, plane - 1)]
            remote(part, part, r_send, r_recv.at[n], sibling).wait_recv()

        @pl.when(n > 0)
        def _():
            part = back.at[pl.ds(from_z * plane, plane)]
            remote(part, part, r_send, r_recv.at[n], sibling).wait_recv()

        for i in range(plane):
            q = from_z * plane + i
            total = beta[q] + back[q].astype(jnp.float32)
            out_ref[0, 0, :, pl.ds(pl.multiple_of(q * LANES, LANES), LANES)] = total.astype(jnp.bfloat16)

    for kind in range(2):
        part = slabs.at[pl.ds(0, nz * ny - 1)]
        remote(part, part, z_send.at[kind], z_recv.at[kind, 0], sibling).wait_send()
    for n in range(7):
        remote(own.at[0], own.at[0], x_send.at[n], sib_recv.at[0], sibling).wait_send()
    part = prod.at[pl.ds(0, chips - 1)]
    remote(part, part, r_send, r_recv.at[0], sibling).wait_send()


def per_device(ny, coeffs, h_blocks, h_cols, g_blocks, g_cols):
    num_blocks = h_cols.shape[1]
    chips = num_blocks // 2
    nz = chips // (2 * ny)
    bf16, dma = jnp.bfloat16, pltpu.SemaphoreType.DMA
    vmem, smem = pl.BlockSpec(memory_space=pltpu.VMEM), pl.BlockSpec(memory_space=pltpu.SMEM)
    hbm = pl.BlockSpec(memory_space=pltpu.HBM)
    return pl.pallas_call(
        functools.partial(kernel, nz, ny),
        out_shape=jax.ShapeDtypeStruct(coeffs.shape, bf16),
        in_specs=[hbm, hbm, smem, hbm, smem],
        out_specs=vmem,
        scratch_shapes=[
            pltpu.VMEM(coeffs.shape[2:], bf16),
            pltpu.VMEM((chips, BLK, LANES), bf16),
            pltpu.VMEM((2, num_blocks, BLK, LANES), bf16),
            pltpu.VMEM((6, nz * ny, BLK, LANES), bf16),
            pltpu.VMEM((4, nz * ny, BLK, LANES), bf16),
            pltpu.VMEM((chips, BLK, LANES), bf16),
            pltpu.VMEM((chips, BLK, LANES), bf16),
            pltpu.VMEM((chips, BLK, LANES), jnp.float32),
            pltpu.VMEM(h_blocks.shape[1:], bf16),
            pltpu.VMEM(g_blocks.shape[1:], bf16),
            dma((3,)), pltpu.SemaphoreType.REGULAR, dma((2,)), dma((2, nz)), dma((7,)), dma((3, nz)), dma((4,)), dma, dma((nz,)),
        ],
        compiler_params=pltpu.CompilerParams(collective_id=0, has_side_effects=True, vmem_limit_bytes=52 * 2**20),
        cost_estimate=pl.CostEstimate(flops=670_000_000, bytes_accessed=9 * 2**20, transcendentals=0),
    )(coeffs, h_blocks, jnp.swapaxes(h_cols, 1, 2), g_blocks, jnp.swapaxes(g_cols, 1, 2))


def solution(mesh, ny=NY):
    return jax.shard_map(
        functools.partial(per_device, ny),
        mesh=mesh,
        in_specs=(
            P("cls", None, "row", None),
            P("cls", None, None, None),
            P("cls", None, None),
            P("cls", None, None, None),
            P("cls", None, None),
        ),
        out_specs=P("cls", None, "row", None),
        check_vma=False,
    )
```
